512 devices in a mesh: row: 16 (over y, core), col: 32 (over z, x).
Axes of the slice: x: 4, y: 8, z: 8, core: 2. Of those that a mesh axis runs over, the one named last changes fastest.
Arguments:
- old_vectors: float32 [8192, 4096], P('row', 'col'), may hold values from -6 to 6, as said below
- pole_values: float32 [8192], replicated, may hold values from 0 to 8192, as said below
- live_mask: int32 [8192], replicated, may hold values from 0 to 1, as said below
- position: int32 [8192], replicated, may hold values from 0 to 8191, as said below
- rank_weight: float32 [1], replicated, may hold values from 0.5 to 2
Outputs:
- new_vectors: float32 [8192, 8192], P('row', 'col')
The draws below stay inside these ranges and needn't reach their ends.
Inputs may be any that keep to these rules, and one draw needn't show every extreme that they name: `pole_values`: strictly increasing; consecutive values differ by 0.2 or more. `old_vectors`: the entries of rows 4095 and 4096 have magnitude 0.5 to 1.5. Each merged position appears exactly once. In every aligned group of 16 consecutive columns s of the halves' eigenvectors (s = h * 4096 + m), exactly 12 have live_mask[position[s]] = 1.
All inputs are finite; a program needn't handle non-finite values.
Results may differ from the reference program's by a relative error of at most 0.0003.
Values sent between devices are 32-bit elements; how exact they have to be, the bound alone decides.
A program may use at most 64 MiB of HBM per device.

```python
import math
import jax
import jax.numpy as jnp
from jax import lax

ORDER = 8192
HALF = 4096
BISECT = 40
DEFL_GROUP = 16
LIVE_GROUP = 12


def draw_old_vectors(key, part):
    main_key = jax.random.fold_in(key, 11)
    sign_key = jax.random.fold_in(key, 12)
    magnitude_key = jax.random.fold_in(key, 13)
    entries = jnp.clip(jax.random.normal(main_key, (ORDER, HALF), jnp.float32), -6.0, 6.0)
    sign_part = jnp.where(jax.random.bernoulli(sign_key, 0.5, (2, HALF)), 1.0, -1.0)
    magnitude = jax.random.uniform(magnitude_key, (2, HALF), jnp.float32, 0.5, 1.5)
    boundary = sign_part * magnitude
    row_index = jnp.arange(ORDER)[:, None]
    entries = jnp.where(row_index == HALF - 1, boundary[0][None, :], entries)
    entries = jnp.where(row_index == HALF, boundary[1][None, :], entries)
    return entries.astype(jnp.float32)


def draw_pole_values(key, part):
    jitter_key = jax.random.fold_in(key, 21)
    jitter = jax.random.uniform(jitter_key, (ORDER,), jnp.float32, 0.0, 0.4)
    return jnp.arange(ORDER).astype(jnp.float32) + jitter


def deflation_tables(key):
    base_key = jax.random.fold_in(key, 31)
    position = jax.random.permutation(jax.random.fold_in(base_key, 1), ORDER).astype(jnp.int32)
    group_count = ORDER // DEFL_GROUP
    scores = jax.random.randint(jax.random.fold_in(base_key, 2), (group_count, DEFL_GROUP), 0, 1048576)
    sort_keys = scores * DEFL_GROUP + jnp.arange(DEFL_GROUP, dtype=jnp.int32)[None, :]
    ranks = jnp.argsort(jnp.argsort(sort_keys, axis=1), axis=1)
    column_live = (ranks >= DEFL_GROUP - LIVE_GROUP).astype(jnp.int32).reshape(ORDER)
    live_mask = jnp.zeros((ORDER,), jnp.int32).at[position].set(column_live)
    return (position, live_mask)


def draw_live_mask(key, part):
    return deflation_tables(key)[1]


def draw_position(key, part):
    return deflation_tables(key)[0]


def setup_inputs(seed: int = 0) -> dict:
    arg_keys = jax.random.split(jax.random.key(seed), 6)
    return {
        "old_vectors": draw_old_vectors(jax.random.fold_in(arg_keys[5], 71), 0),
        "pole_values": draw_pole_values(jax.random.fold_in(arg_keys[5], 71), 0),
        "live_mask": draw_live_mask(jax.random.fold_in(arg_keys[5], 71), 0),
        "position": draw_position(jax.random.fold_in(arg_keys[5], 71), 0),
        "rank_weight": jnp.clip(jnp.exp(jax.random.uniform(arg_keys[4], (1,), jnp.float32, math.log(0.5), math.log(2.0))), 0.5, 2.0),
    }


def bracket_lengths(pole_values, live_mask, squares, rank_value):
    order_size = pole_values.shape[0]
    positions = jnp.arange(order_size, dtype=jnp.int32)
    marked = jnp.where(live_mask > 0, positions, order_size).astype(jnp.int32)
    shifted = jnp.concatenate([marked[1:], jnp.full((1,), order_size, jnp.int32)])
    following = lax.cummin(shifted, axis=0, reverse=True)
    weight_sum = rank_value * jnp.sum(squares)
    next_gap = pole_values[jnp.minimum(following, order_size - 1)] - pole_values
    return jnp.where(following < order_size, next_gap, weight_sum)

def bisect_roots(pole_here, bracket_len, pole_values, squares, live_mask, rank_value):
    pole_diff = pole_values[None, :] - pole_here[:, None]
    alive_cols = (live_mask > 0)[None, :]

    def halving(interval, unused):
        low_end, high_end = interval
        middle = 0.5 * (low_end + high_end)
        offset_gap = pole_diff - middle[:, None]
        summands = jnp.where(alive_cols, squares[None, :] / jnp.where(alive_cols, offset_gap, 1.0), 0.0)
        secular = 1.0 + rank_value * lax.optimization_barrier(jnp.sum(summands, axis=1))
        is_below = secular < 0.0
        return ((jnp.where(is_below, middle, low_end), jnp.where(is_below, high_end, middle)), None)
    interval, unused = lax.scan(halving, (jnp.zeros_like(bracket_len), bracket_len), None, length=BISECT)
    return 0.5 * (interval[0] + interval[1])

def log_terms(pole_here, offsets, live_here, own_index, pole_values, live_mask):
    order_size = pole_values.shape[0]
    pole_diff = pole_values[None, :] - pole_here[:, None]
    on_pole = own_index[:, None] == jnp.arange(order_size, dtype=jnp.int32)[None, :]
    quotient = jnp.where(on_pole, offsets[:, None], 1.0 - offsets[:, None] / jnp.where(on_pole, 1.0, pole_diff))
    in_play = (live_here[:, None] > 0) & (live_mask[None, :] > 0)
    logs = jnp.where(in_play, jnp.log(jnp.abs(jnp.where(in_play, quotient, 1.0))), 0.0)
    return lax.optimization_barrier(jnp.sum(logs, axis=0))

def column_norms(pole_here, offsets, live_here, pole_values, live_mask, hat_weights):
    alive_cols = (live_mask > 0)[None, :]
    offset_gap = pole_values[None, :] - pole_here[:, None] - offsets[:, None]
    summands = jnp.where(alive_cols, hat_weights[None, :] ** 2 / jnp.where(alive_cols, offset_gap, 1.0) ** 2, 0.0)
    return jnp.where(live_here > 0, jnp.sqrt(lax.optimization_barrier(jnp.sum(summands, axis=1))), 1.0)

def cauchy_tile(sorted_rows, pole_cols, offset_cols, norm_cols, live_cols, col_index, pole_values, live_mask, hat_weights):
    row_poles = pole_values[sorted_rows]
    row_hats = hat_weights[sorted_rows]
    row_live = live_mask[sorted_rows] > 0
    col_live = (live_cols > 0)[None, :]
    both_live = row_live[:, None] & col_live
    offset_gap = row_poles[:, None] - pole_cols[None, :] - offset_cols[None, :]
    entries = row_hats[:, None] / jnp.where(both_live, offset_gap, 1.0) / norm_cols[None, :]
    identity = (sorted_rows[:, None] == col_index[None, :]).astype(jnp.float32)
    return jnp.where(col_live, jnp.where(both_live, entries, 0.0), identity)

def reference(old_vectors, pole_values, live_mask, position, rank_weight):
    rank_value = rank_weight[0]
    boundary = jnp.concatenate([old_vectors[HALF - 1], old_vectors[HALF]])
    spread = jnp.zeros((ORDER,), old_vectors.dtype).at[position].set(boundary)
    coupling = jnp.where(live_mask > 0, spread, 0.0)
    squares = coupling * coupling
    bracket_len = bracket_lengths(pole_values, live_mask, squares, rank_value)
    groups = ORDER // 512
    index_all = jnp.arange(ORDER, dtype=jnp.int32)
    grouped = (pole_values.reshape(groups, 512), bracket_len.reshape(groups, 512), live_mask.reshape(groups, 512), index_all.reshape(groups, 512))

    def solve_group(members):
        bisected = bisect_roots(members[0], members[1], pole_values, squares, live_mask, rank_value)
        return jnp.where(members[2] > 0, bisected, 0.5 * members[1])
    offsets = lax.map(solve_group, grouped).reshape(ORDER)
    offset_groups = offsets.reshape(groups, 512)

    def log_group(members):
        return log_terms(members[0], members[1], members[2], members[3], pole_values, live_mask)
    log_sum = lax.optimization_barrier(jnp.sum(lax.map(log_group, (grouped[0], offset_groups, grouped[2], grouped[3])), axis=0))
    hat_weights = jnp.where(live_mask > 0, jnp.sign(coupling) * jnp.exp(0.5 * (log_sum - jnp.log(rank_value))), 0.0)

    def norm_group(members):
        return column_norms(members[0], members[1], members[2], pole_values, live_mask, hat_weights)
    norms = lax.map(norm_group, (grouped[0], offset_groups, grouped[2])).reshape(ORDER)

    def column_group(members):
        cauchy = cauchy_tile(position, members[0], members[1], members[2], members[3], members[4], pole_values, live_mask, hat_weights)
        top_rows = jnp.dot(old_vectors[:HALF], cauchy[:HALF], precision=lax.Precision.HIGHEST, preferred_element_type=jnp.float32)
        bottom_rows = jnp.dot(old_vectors[HALF:], cauchy[HALF:], precision=lax.Precision.HIGHEST, preferred_element_type=jnp.float32)
        return jnp.concatenate([top_rows, bottom_rows])
    stacked = lax.map(column_group, (grouped[0], offset_groups, norms.reshape(groups, 512), grouped[2], grouped[3]))
    return jnp.transpose(stacked, (1, 0, 2)).reshape(ORDER, ORDER)
```

```python
import functools

import jax
import jax.numpy as jnp
from jax import lax
from jax.experimental import pallas as pl
from jax.experimental.pallas import tpu as pltpu
from jax.sharding import PartitionSpec as P

F32 = jnp.float32
BF16 = jnp.bfloat16
MESH = pl.DeviceIdType.MESH
FAR = 1e30
FAR_TEST = 1e29
ROOT_STEPS = 7
NR, NC, NZ, NX = 16, 32, 8, 4
ROWS, COLS = 512, 128
OUT = 256
OWN = OUT // NR
HALF_ROWS = ROWS // 2


def reciprocal(x):
    r = pl.reciprocal(x, approx=True)
    r = r * (2.0 - x * r)
    return r * (2.0 - x * r)


def kernel(
    x_ref, pole_ref, live_ref, posn_ref, rank_ref, out_ref,
    panel, buf1, buf2, buf3, buf4, buf5,
    djb, ljb, kp, kd, kl, npole, nsq, nsg, dd, bracket_ref,
    ah, al, ch, cl, tx, rx, norm_ref,
    s1, s2s, s2r, s3s, s3r, s4s, s4r, s5s, s5r,
    own_sem, os, orr, xs, xr, zs, zr, rs, rr, s1s,
):
    r = lax.axis_index("row")
    c = lax.axis_index("col")
    z = c // NX
    x = lax.rem(c, NX)
    h = r // (NR // 2)
    rho = rank_ref[0]

    def col_dev(dz, dx):
        return (r, lax.rem(z + dz + NZ, NZ) * NX + lax.rem(x + dx + NX, NX))

    barrier = pltpu.get_barrier_semaphore()
    for k in range(1, NC):
        pl.semaphore_signal(barrier, inc=1, device_id=(r, lax.rem(c + k, NC)), device_id_type=MESH)
    for k in range(1, NR):
        pl.semaphore_signal(barrier, inc=1, device_id=(lax.rem(r + k, NR), c), device_id_type=MESH)

    own_copy = pltpu.make_async_copy(x_ref, panel.at[0, z], own_sem)
    own_copy.start()

    for q in range(2):
        prow = pole_ref[pl.ds(2 * c + q, 1), :]
        djb[q * 128:(q + 1) * 128, :] = jnp.transpose(jnp.broadcast_to(prow, (128, 128)))
        lrow = live_ref[pl.ds(2 * c + q, 1), :].astype(F32)
        ljb[q * 128:(q + 1) * 128, :] = jnp.transpose(jnp.broadcast_to(lrow, (128, 128)))

    pos = jnp.concatenate(
        [posn_ref[pl.ds(c, 1), :], posn_ref[pl.ds(NC + c, 1), :]], axis=1
    )
    table = jnp.transpose(pole_ref[...])
    t0 = table.astype(BF16)
    rest = table - t0.astype(F32)
    t1 = rest.astype(BF16)
    t2 = (rest - t1.astype(F32)).astype(BF16)
    tl = jnp.transpose(live_ref[...].astype(F32)).astype(BF16)
    tables = jnp.concatenate([t0, t1, t2, tl], axis=0)
    high = lax.broadcasted_iota(jnp.int32, (64, 256), 0) == (pos >> 7)
    picked = jnp.dot(tables, jnp.where(high, 1.0, 0.0).astype(BF16), preferred_element_type=F32)
    low = lax.broadcasted_iota(jnp.int32, (128, 256), 0) == (pos & 127)
    pole_s = jnp.sum(
        jnp.where(low, (picked[0:128] + picked[128:256]) + picked[256:384], 0.0), axis=0, keepdims=True
    )
    live_s = jnp.sum(jnp.where(low, picked[384:512], 0.0), axis=0, keepdims=True)
    buf2[c, :, :] = jnp.zeros((8, 128), F32)
    buf2[c, 2:3, :] = pole_s[:, 0:128]
    buf2[c, 3:4, :] = pole_s[:, 128:256]
    buf2[c, 4:5, :] = live_s[:, 0:128]
    buf2[c, 5:6, :] = live_s[:, 128:256]

    pl.semaphore_wait(barrier, NR - 1 + NC - 1)

    def boundary_copy(q, k):
        src = x_ref.at[pl.ds(ROWS - 8, 8)] if q == 0 else x_ref.at[pl.ds(0, 8)]
        return pltpu.make_async_remote_copy(
            src_ref=src, dst_ref=buf1.at[q], send_sem=s1s.at[k - 1], recv_sem=s1.at[q],
            device_id=(lax.rem(r + k, NR), c), device_id_type=MESH,
        )

    for q, owner in ((0, NR // 2 - 1), (1, NR // 2)):
        @pl.when(r == owner)
        def _():
            for k in range(1, NR):
                boundary_copy(q, k).start()
            buf1[q, :, :] = x_ref[ROWS - 8:ROWS, :] if q == 0 else x_ref[0:8, :]

    up, down = col_dev(1, 0), col_dev(-1, 0)
    across = col_dev(0, 2)

    def part(k):
        return pl.ds(k * HALF_ROWS, HALF_ROWS)

    def own_line(d, s, k):
        block = lax.rem(z - s + NZ, NZ) if d == 0 else lax.rem(z + s, NZ)
        src = x_ref.at[part(k)] if s == 0 else panel.at[0, block, part(k)]
        return pltpu.make_async_remote_copy(
            src_ref=src, dst_ref=panel.at[0, block, part(k)], send_sem=os.at[d, s, k],
            recv_sem=orr.at[d, s, k], device_id=up if d == 0 else down, device_id_type=MESH,
        )

    def over_x(i, k):
        block = lax.rem(z + (0, -1, 1)[i] + NZ, NZ)
        src = x_ref.at[part(k)] if i == 0 else panel.at[0, block, part(k)]
        return pltpu.make_async_remote_copy(
            src_ref=src, dst_ref=panel.at[1, block, part(k)], send_sem=xs.at[i, k],
            recv_sem=xr.at[i, k], device_id=across, device_id_type=MESH,
        )

    def x_line(d, s, k):
        block = lax.rem(z - s + NZ, NZ) if d == 0 else lax.rem(z + s, NZ)
        return pltpu.make_async_remote_copy(
            src_ref=panel.at[1, block, part(k)], dst_ref=panel.at[1, block, part(k)],
            send_sem=zs.at[d, s - 1, k], recv_sem=zr.at[d, s - 1, k],
            device_id=up if d == 0 else down, device_id_type=MESH,
        )

    for k in range(2):
        for d in range(2):
            own_line(d, 0, k).start()
        over_x(0, k).start()

    @pl.when(r != NR // 2 - 1)
    def _():
        boundary_copy(0, 1).wait_recv()

    @pl.when(r != NR // 2)
    def _():
        boundary_copy(1, 1).wait_recv()

    buf2[c, 0:1, :] = buf1[0, 7:8, :]
    buf2[c, 1:2, :] = buf1[1, 0:1, :]

    def spread(buf, n, send, recv, along_row):
        me = r if along_row else c
        order = sorted(range(1, n), key=lambda k: -min(k, n - k))
        for k in order:
            peer = lax.rem(me + k, n)
            pltpu.make_async_remote_copy(
                src_ref=buf.at[me], dst_ref=buf.at[me], send_sem=send, recv_sem=recv,
                device_id=(peer, c) if along_row else (r, peer), device_id_type=MESH,
            ).start()

    def settle(buf, n, sem):
        some = buf.at[pl.ds(0, n - 1)]
        pltpu.make_async_copy(some, some, sem).wait()

    spread(buf2, NC, s2s, s2r, False)

    own_first = pl.multiple_of(r * OWN, OWN)
    dj = djb[pl.ds(own_first, OWN), :]
    nearest = jnp.full((OWN, 128), FAR, F32)
    for k in range(64):
        apole = jnp.where(live_ref[k:k + 1, :] > 0, pole_ref[k:k + 1, :], FAR)
        gap = apole - dj
        nearest = jnp.minimum(nearest, jnp.where(gap > 0.0, gap, FAR))
    bracket_ref[...] = jnp.broadcast_to(jnp.min(nearest, axis=1, keepdims=True), (OWN, 128))

    for k in range(2):
        for d in range(2):
            own_line(d, 0, k).wait_recv()
            own_line(d, 1, k).start()
        for i in (1, 2):
            over_x(i, k).start()

    settle(buf2, NC, s2r)

    bound = jnp.concatenate([buf2[:, 0, :], buf2[:, 1, :]], axis=0)
    praw = jnp.concatenate([buf2[:, 2, :], buf2[:, 3, :]], axis=0)
    alive = jnp.concatenate([buf2[:, 4, :], buf2[:, 5, :]], axis=0) > 0.5
    coupling = jnp.where(alive, bound, 0.0)
    nsq[...] = coupling * coupling
    nsg[...] = jnp.where(coupling > 0.0, 1.0, jnp.where(coupling < 0.0, -1.0, 0.0))
    npole[...] = jnp.where(alive, praw, FAR)

    weight_sum = rho * jnp.sum(nsq[...], axis=(0, 1), keepdims=True)
    near = bracket_ref[:, 0:1]
    bracket = jnp.where(near < FAR_TEST, near, weight_sum)
    for k in range(64):
        dd[:, k * 128:(k + 1) * 128] = npole[k:k + 1, :] - dj

    def root_step(_, carry):
        t, lo, hi = carry
        tb = jnp.broadcast_to(t, (OWN, 128))
        zero = jnp.zeros((OWN, 128), F32)
        psi, phi, dpsi, dphi = zero, zero, zero, zero
        for k in range(64):
            q = reciprocal(dd[:, k * 128:(k + 1) * 128] - tb)
            w = nsq[k:k + 1, :] * q
            dw = w * q
            below = w < 0.0
            psi = psi + jnp.where(below, w, 0.0)
            phi = phi + jnp.where(below, 0.0, w)
            dpsi = dpsi + jnp.where(below, dw, 0.0)
            dphi = dphi + jnp.where(below, 0.0, dw)
        psi = jnp.sum(psi, axis=1, keepdims=True)
        phi = jnp.sum(phi, axis=1, keepdims=True)
        dpsi = jnp.sum(dpsi, axis=1, keepdims=True)
        dphi = jnp.sum(dphi, axis=1, keepdims=True)
        secular = 1.0 + rho * (psi + phi)
        is_below = secular < 0.0
        lo = jnp.where(is_below, t, lo)
        hi = jnp.where(is_below, hi, t)
        e = bracket - t
        lower = rho * t * t * dpsi
        upper = rho * e * e * dphi
        level = 1.0 + rho * ((psi + t * dpsi) + (phi - e * dphi))
        linear = level * bracket + lower + upper
        constant = lower * bracket
        side = level * bracket - lower + upper
        spread_root = jnp.sqrt(side * side + 4.0 * lower * upper)
        positive = linear > 0.0
        top = jnp.where(positive, 2.0 * constant, linear - spread_root)
        under = jnp.where(positive, linear + spread_root, 2.0 * level)
        fresh = top / jnp.where(under == 0.0, 1.0, under)
        usable = (fresh > 0.0) & (fresh < bracket)
        fresh = jnp.where(usable, jnp.minimum(jnp.maximum(fresh, lo), hi), 0.5 * (lo + hi))
        return fresh, lo, hi

    start = 0.5 * bracket
    root, _, _ = lax.fori_loop(0, ROOT_STEPS, root_step, (start, jnp.zeros_like(start), bracket))
    own_live = ljb[pl.ds(own_first, OWN), :] > 0.5
    buf3[r, :, :] = jnp.where(own_live, jnp.broadcast_to(root, (OWN, 128)), jnp.broadcast_to(start, (OWN, 128)))
    spread(buf3, NR, s3s, s3r, True)

    for k in range(2):
        for d in range(2):
            own_line(d, 1, k).wait_recv()
            own_line(d, 2, k).start()

    settle(buf3, NR, s3r)

    for i in range(4):
        poles = npole[pl.ds(4 * r + i, 1), :]
        total = jnp.ones((8, 128), F32)
        for g in range(OUT // 8):
            d_j = djb[g * 8:(g + 1) * 8, :]
            off = buf3[g // 2, (g % 2) * 8:(g % 2) * 8 + 8, :]
            gap = poles - d_j
            ratio = (gap - off) * reciprocal(jnp.where(gap == 0.0, 1.0, gap))
            total = total * jnp.where(ljb[g * 8:(g + 1) * 8, :] > 0.5, jnp.abs(ratio), 1.0)
        total = total[0:4] * total[4:8]
        total = total[0:2] * total[2:4]
        buf4[c, i:i + 1, :] = total[0:1] * total[1:2]
    for q in range(2):
        tile = jnp.concatenate([buf3[q * 8 + g, :, :] for g in range(8)], axis=0)
        buf4[c, 4 + q:5 + q, :] = jnp.transpose(tile)[0:1, :]
    buf4[c, 6:8, :] = jnp.ones((2, 128), F32)
    spread(buf4, NC, s4s, s4r, False)

    own_line(0, 2, 0).wait_recv()
    own_line(0, 3, 0).start()
    own_line(1, 2, 1).wait_recv()
    own_line(1, 3, 1).start()
    for k in range(2):
        for d in range(2):
            over_x(1 + d, k).wait_recv()
            x_line(d, 1, k).start()
    own_line(0, 2, 1).wait_recv()
    own_line(1, 2, 0).wait_recv()

    for b in range(16):
        line = lax.rem(x + 2 * (b // 8), NX)
        source = (b % 8) * NX + line
        row = h * NC + source
        alive_row = buf2[source, pl.ds(4 + h, 1), :] > 0.5
        kp[b:b + 1, :] = npole[pl.ds(row, 1), :]
        place = posn_ref[pl.ds(row, 1), :].astype(F32)
        kd[b:b + 1, :] = jnp.where(alive_row, -1.0, place)
    kp[16:128, :] = jnp.zeros((112, 128), F32)
    kd[16:128, :] = jnp.zeros((112, 128), F32)
    kpt = jnp.transpose(kp[...])
    kdt = jnp.transpose(kd[...])
    kp[...] = kpt
    kd[...] = kdt

    def inverse_gaps(group, block, offs):
        for q in range(2):
            d_j = pole_ref[pl.ds(2 * block + q, 1), :]
            alive_j = live_ref[pl.ds(2 * block + q, 1), :] > 0
            off = offs[q]
            index = (lax.broadcasted_iota(jnp.int32, (1, 128), 1) + (block * OUT + q * 128)).astype(F32)
            for b in range(16):
                col = kp[:, b:b + 1]
                gap = (col - d_j) - off
                inverse = jnp.where(col < FAR_TEST, reciprocal(gap), 0.0)
                same = jnp.where(kd[:, b:b + 1] == index, 1.0, 0.0)
                value = jnp.where(alive_j, inverse, same)
                hi = value.astype(BF16)
                lo = (value - hi.astype(F32)).astype(BF16)
                ch[b * 128:(b + 1) * 128, group * OUT + q * 128:group * OUT + (q + 1) * 128] = hi
                cl[b * 128:(b + 1) * 128, group * OUT + q * 128:group * OUT + (q + 1) * 128] = lo

    settle(buf4, NC, s4r)
    product = buf4[0, :, :]
    for k in range(1, NC):
        product = product * buf4[k, :, :]
    first_rows = lax.broadcasted_iota(jnp.int32, (8, 128), 0) < 4
    product = jnp.where(first_rows, product, 1.0)
    buf5[r, :, :] = jnp.sqrt(product / rho)
    spread(buf5, NR, s5s, s5r, True)

    for k in range(2):
        for d in range(2):
            x_line(d, 1, k).wait_recv()
            x_line(d, 2, k).start()

    right = z * NX + lax.rem(x + 1, NX)
    left = z * NX + lax.rem(x + NX - 1, NX)
    for group, block in ((0, c), (1, right), (2, left)):
        inverse_gaps(group, block, [buf4[block, 4:5, :], buf4[block, 5:6, :]])

    settle(buf5, NR, s5r)

    def scaled(b):
        line = lax.rem(x + 2 * (b // 8), NX)
        row = h * NC + (b % 8) * NX + line
        hat = buf5[h * 8 + b % 8, pl.ds(line, 1), :] * nsg[pl.ds(row, 1), :]
        hat = jnp.where(npole[pl.ds(row, 1), :] < FAR_TEST, hat, 1.0)
        value = panel[b // 8, b % 8, :, :] * hat
        hi = value.astype(BF16)
        ah[:, b * 128:(b + 1) * 128] = hi
        al[:, b * 128:(b + 1) * 128] = (value - hi.astype(F32)).astype(BF16)

    own_copy.wait()
    own_line(0, 3, 0).wait_recv()
    own_line(1, 3, 1).wait_recv()
    for b in range(8):
        scaled(b)

    over_x(0, 0).wait_recv()
    over_x(0, 1).wait_recv()
    x_line(0, 2, 0).wait_recv()
    x_line(0, 3, 0).start()
    x_line(1, 2, 1).wait_recv()
    x_line(1, 3, 1).start()
    x_line(0, 2, 1).wait_recv()
    x_line(1, 2, 0).wait_recv()
    x_line(0, 3, 0).wait_recv()
    x_line(1, 3, 1).wait_recv()
    for b in range(8, 16):
        scaled(b)

    def product_of(first, count, group):
        rows = slice(first, first + count)
        cols = slice(group * OUT, (group + 1) * OUT)
        a_hi, a_lo = ah[rows, :], al[rows, :]
        c_hi, c_lo = ch[:, cols], cl[:, cols]
        return (
            jnp.dot(a_hi, c_lo, preferred_element_type=F32)
            + jnp.dot(a_lo, c_hi, preferred_element_type=F32)
        ) + jnp.dot(a_hi, c_hi, preferred_element_type=F32)

    def partial_copy(side):
        return pltpu.make_async_remote_copy(
            src_ref=tx.at[side], dst_ref=rx.at[side], send_sem=rs.at[side], recv_sem=rr.at[side],
            device_id=col_dev(0, 1 if side == 0 else -1), device_id_type=MESH,
        )

    for side in range(2):
        tx[side, :, :] = product_of(side * HALF_ROWS, HALF_ROWS, 1 + side)
        partial_copy(side).start()
    for side in range(2):
        out_ref[side * HALF_ROWS:(side + 1) * HALF_ROWS, :] = product_of(side * HALF_ROWS, HALF_ROWS, 0)

    def norm_group(g, _):
        first = pl.multiple_of(g * 8, 8)
        d_j = djb[pl.ds(first, 8), :]
        off = buf3[g // 2, pl.ds(pl.multiple_of(lax.rem(g, 2) * 8, 8), 8), :]
        total = jnp.zeros((8, 128), F32)
        for k in range(64):
            poles = npole[k:k + 1, :]
            hat = jnp.where(poles < FAR_TEST, buf5[k // 4, k % 4:k % 4 + 1, :], 0.0)
            w = hat * reciprocal((poles - d_j) - off)
            total = total + w * w
        norm_ref[pl.ds(first, 8), :] = total
        return 0

    lax.fori_loop(0, OUT // 8, norm_group, 0)
    scales = []
    for q in range(2):
        square = jnp.sum(jnp.transpose(norm_ref[q * 128:(q + 1) * 128, :]), axis=0, keepdims=True)
        alive_j = live_ref[pl.ds(2 * c + q, 1), :] > 0
        scales.append(jnp.where(alive_j, 1.0 / jnp.sqrt(jnp.where(alive_j, square, 1.0)), 1.0))
    scale = jnp.concatenate(scales, axis=1)

    for side in range(2):
        partial_copy(side).wait_recv()
        rows = slice(side * HALF_ROWS, (side + 1) * HALF_ROWS)
        out_ref[rows, :] = (out_ref[rows, :] + rx[side, :, :]) * scale

    for q, owner in ((0, NR // 2 - 1), (1, NR // 2)):
        @pl.when(r == owner)
        def _():
            for k in range(1, NR):
                boundary_copy(q, k).wait_send()

    settle(buf2, NC, s2s)
    settle(buf3, NR, s3s)
    settle(buf4, NC, s4s)
    settle(buf5, NR, s5s)
    for s in range(3):
        for k in range(2):
            over_x(s, k).wait_send()
            for d in range(2):
                own_line(d, s, k).wait_send()
    for s in (1, 2):
        for k in range(2):
            for d in range(2):
                x_line(d, s, k).wait_send()
    for d in range(2):
        own_line(d, 3, d).wait_send()
        x_line(d, 3, d).wait_send()
        partial_copy(d).wait_send()


def shards(old_vectors, pole_values, live_mask, position, rank_weight):
    vmem = pl.BlockSpec(memory_space=pltpu.VMEM)
    v = pltpu.VMEM
    dma = pltpu.SemaphoreType.DMA
    one = dma(())
    return pl.pallas_call(
        kernel,
        out_shape=jax.ShapeDtypeStruct((ROWS, OUT), F32),
        in_specs=[vmem] * 4 + [pl.BlockSpec(memory_space=pltpu.SMEM)],
        out_specs=vmem,
        scratch_shapes=[
            v((2, NZ, ROWS, COLS), F32),
            v((2, 8, 128), F32), v((NC, 8, 128), F32), v((NR, OWN, 128), F32),
            v((NC, 8, 128), F32), v((NR, 8, 128), F32),
            v((OUT, 128), F32), v((OUT, 128), F32),
            v((128, 128), F32), v((128, 128), F32), v((8, 128), F32),
            v((64, 128), F32), v((64, 128), F32), v((64, 128), F32),
            v((OWN, 8192), F32), v((OWN, 128), F32),
            v((ROWS, 2048), BF16), v((ROWS, 2048), BF16),
            v((2048, 3 * OUT), BF16), v((2048, 3 * OUT), BF16),
            v((2, HALF_ROWS, OUT), F32), v((2, HALF_ROWS, OUT), F32), v((OUT, 128), F32),
            dma((2,)), one, one, one, one, one, one, one, one,
            one, dma((2, 4, 2)), dma((2, 4, 2)), dma((3, 2)), dma((3, 2)),
            dma((2, 3, 2)), dma((2, 3, 2)), dma((2,)), dma((2,)), dma((NR - 1,)),
        ],
        compiler_params=pltpu.CompilerParams(
            collective_id=0, has_side_effects=True, vmem_limit_bytes=56 * 2**20
        ),
    )(
        old_vectors,
        pole_values.reshape(64, 128),
        live_mask.reshape(64, 128),
        position.reshape(64, 128),
        rank_weight,
    )


def solution(mesh):
    in_specs = (P("row", "col"), P(), P(), P(), P())
    return jax.shard_map(
        shards, mesh=mesh, in_specs=in_specs, out_specs=P("row", "col"), check_vma=False
    )
```

```python
import functools

import jax
import jax.numpy as jnp
from jax import lax
from jax.experimental import pallas as pl
from jax.experimental.pallas import tpu as pltpu
from jax.sharding import PartitionSpec as P

F32 = jnp.float32
BF16 = jnp.bfloat16
MESH = pl.DeviceIdType.MESH
FAR = 1e30
FAR_TEST = 1e29
ROUGH_STEPS, FINE_STEPS = 4, 3
NR, NC, NZ, NX = 16, 32, 8, 4
ROWS, COLS = 512, 128
OUT = 256
OWN = OUT // NR
HALF_ROWS = ROWS // 2
PIECE = HALF_ROWS // 2


def reciprocal(x):
    r = pl.reciprocal(x, approx=True)
    return r * (2.0 - x * r)


def peers(me, n):
    minor, major = (2, NR // 2) if n == NR else (NX, NZ)
    steps = [(a, b) for a in range(major) for b in range(minor) if a or b]
    steps.sort(key=lambda ab: -2 * min(ab[0], major - ab[0]) - min(ab[1], minor - ab[1]))
    return [
        lax.rem(me // minor + a, major) * minor + lax.rem(lax.rem(me, minor) + b, minor)
        for a, b in steps
    ]


def kernel(
    x_ref, pole_ref, live_ref, posn_ref, rank_ref, out_ref,
    panel, buf1, buf2, buf3, buf4, buf5,
    djb, ljb, kp, kd, kl, npole, nsq, nsg, dd, bracket_ref,
    ah, al, ch, cl, tx, rx, norm_ref, sq_ref,
    s1, s2s, s2r, s3s, s3r, s4s, s4r, s5s, s5r,
    own_sem, os, orr, xs, xr, zs, zr, rs, rr, s1s,
):
    r = lax.axis_index("row")
    c = lax.axis_index("col")
    z = c // NX
    x = lax.rem(c, NX)
    h = r // (NR // 2)
    rho = rank_ref[0]

    def col_dev(dz, dx):
        return (r, lax.rem(z + dz + NZ, NZ) * NX + lax.rem(x + dx + NX, NX))

    barrier = pltpu.get_barrier_semaphore()
    for peer in peers(c, NC):
        pl.semaphore_signal(barrier, inc=1, device_id=(r, peer), device_id_type=MESH)
    for peer in peers(r, NR):
        pl.semaphore_signal(barrier, inc=1, device_id=(peer, c), device_id_type=MESH)

    own_copy = pltpu.make_async_copy(x_ref, panel.at[0, z], own_sem)
    own_copy.start()

    for q in range(2):
        prow = pole_ref[pl.ds(2 * c + q, 1), :]
        djb[q * 128:(q + 1) * 128, :] = jnp.transpose(jnp.broadcast_to(prow, (128, 128)))
        lrow = live_ref[pl.ds(2 * c + q, 1), :].astype(F32)
        ljb[q * 128:(q + 1) * 128, :] = jnp.transpose(jnp.broadcast_to(lrow, (128, 128)))

    pos = jnp.concatenate(
        [posn_ref[pl.ds(c, 1), :], posn_ref[pl.ds(NC + c, 1), :]], axis=1
    )
    table = jnp.transpose(pole_ref[...])
    t0 = table.astype(BF16)
    rest = table - t0.astype(F32)
    t1 = rest.astype(BF16)
    t2 = (rest - t1.astype(F32)).astype(BF16)
    tl = jnp.transpose(live_ref[...].astype(F32)).astype(BF16)
    tables = jnp.concatenate([t0, t1, t2, tl], axis=0)
    high = lax.broadcasted_iota(jnp.int32, (64, 256), 0) == (pos >> 7)
    picked = jnp.dot(tables, jnp.where(high, 1.0, 0.0).astype(BF16), preferred_element_type=F32)
    low = lax.broadcasted_iota(jnp.int32, (128, 256), 0) == (pos & 127)
    pole_s = jnp.sum(
        jnp.where(low, (picked[0:128] + picked[128:256]) + picked[256:384], 0.0), axis=0, keepdims=True
    )
    live_s = jnp.sum(jnp.where(low, picked[384:512], 0.0), axis=0, keepdims=True)
    buf2[c, :, :] = jnp.zeros((8, 128), F32)
    buf2[c, 2:3, :] = pole_s[:, 0:128]
    buf2[c, 3:4, :] = pole_s[:, 128:256]
    buf2[c, 4:5, :] = live_s[:, 0:128]
    buf2[c, 5:6, :] = live_s[:, 128:256]

    pl.semaphore_wait(barrier, NR - 1 + NC - 1)

    def boundary_copy(q, k):
        src = x_ref.at[pl.ds(ROWS - 8, 8)] if q == 0 else x_ref.at[pl.ds(0, 8)]
        return pltpu.make_async_remote_copy(
            src_ref=src, dst_ref=buf1.at[q], send_sem=s1s.at[k - 1], recv_sem=s1.at[q],
            device_id=(peers(r, NR)[k - 1], c), device_id_type=MESH,
        )

    for q, owner in ((0, NR // 2 - 1), (1, NR // 2)):
        @pl.when(r == owner)
        def _():
            for k in range(1, NR):
                boundary_copy(q, k).start()
            buf1[q, :, :] = x_ref[ROWS - 8:ROWS, :] if q == 0 else x_ref[0:8, :]

    up, down = col_dev(1, 0), col_dev(-1, 0)
    across = col_dev(0, 2)

    def part(k):
        return pl.ds(k * HALF_ROWS, HALF_ROWS)

    def own_line(d, s, k):
        block = lax.rem(z - s + NZ, NZ) if d == 0 else lax.rem(z + s, NZ)
        src = x_ref.at[part(k)] if s == 0 else panel.at[0, block, part(k)]
        return pltpu.make_async_remote_copy(
            src_ref=src, dst_ref=panel.at[0, block, part(k)], send_sem=os.at[d, s, k],
            recv_sem=orr.at[d, s, k], device_id=up if d == 0 else down, device_id_type=MESH,
        )

    def over_x(i, k):
        block = lax.rem(z + (0, -1, 1, -2, 2)[i] + NZ, NZ)
        src = x_ref.at[part(k)] if i == 0 else panel.at[0, block, part(k)]
        return pltpu.make_async_remote_copy(
            src_ref=src, dst_ref=panel.at[1, block, part(k)], send_sem=xs.at[i, k],
            recv_sem=xr.at[i, k], device_id=across, device_id_type=MESH,
        )

    def x_line(d, s, k):
        block = lax.rem(z - s + NZ, NZ) if d == 0 else lax.rem(z + s, NZ)
        return pltpu.make_async_remote_copy(
            src_ref=panel.at[1, block, part(k)], dst_ref=panel.at[1, block, part(k)],
            send_sem=zs.at[d, s - 1, k], recv_sem=zr.at[d, s - 1, k],
            device_id=up if d == 0 else down, device_id_type=MESH,
        )

    for k in range(2):
        for d in range(2):
            own_line(d, 0, k).start()
        over_x(0, k).start()

    @pl.when(r != NR // 2 - 1)
    def _():
        boundary_copy(0, 1).wait_recv()

    @pl.when(r != NR // 2)
    def _():
        boundary_copy(1, 1).wait_recv()

    buf2[c, 0:1, :] = buf1[0, 7:8, :]
    buf2[c, 1:2, :] = buf1[1, 0:1, :]

    def spread(buf, n, send, recv, along_row):
        me = r if along_row else c
        for peer in peers(me, n):
            pltpu.make_async_remote_copy(
                src_ref=buf.at[me], dst_ref=buf.at[me], send_sem=send, recv_sem=recv,
                device_id=(peer, c) if along_row else (r, peer), device_id_type=MESH,
            ).start()

    def settle(buf, n, sem):
        some = buf.at[pl.ds(0, n - 1)]
        pltpu.make_async_copy(some, some, sem).wait()

    spread(buf2, NC, s2s, s2r, False)

    own_first = pl.multiple_of(r * OWN, OWN)
    dj = djb[pl.ds(own_first, OWN), :]
    nearest = jnp.full((OWN, 128), FAR, F32)
    for k in range(64):
        apole = jnp.where(live_ref[k:k + 1, :] > 0, pole_ref[k:k + 1, :], FAR)
        gap = apole - dj
        nearest = jnp.minimum(nearest, jnp.where(gap > 0.0, gap, FAR))
    bracket_ref[...] = jnp.broadcast_to(jnp.min(nearest, axis=1, keepdims=True), (OWN, 128))

    for second in range(2):
        for d in range(2):
            k = d ^ second
            own_line(d, 0, k).wait_recv()
            own_line(d, 1, k).start()
            over_x(1 + d, k).start()
    for d in range(2):
        own_line(d, 1, d).wait_recv()
        own_line(d, 2, d).start()
        over_x(3 + d, d).start()

    settle(buf2, NC, s2r)

    bound = jnp.concatenate([buf2[:, 0, :], buf2[:, 1, :]], axis=0)
    praw = jnp.concatenate([buf2[:, 2, :], buf2[:, 3, :]], axis=0)
    alive = jnp.concatenate([buf2[:, 4, :], buf2[:, 5, :]], axis=0) > 0.5
    coupling = jnp.where(alive, bound, 0.0)
    nsq[...] = coupling * coupling
    nsg[...] = jnp.where(coupling > 0.0, 1.0, jnp.where(coupling < 0.0, -1.0, 0.0))
    npole[...] = jnp.where(alive, praw, FAR)

    weight_sum = rho * jnp.sum(nsq[...], axis=(0, 1), keepdims=True)
    near = bracket_ref[:, 0:1]
    bracket = jnp.where(near < FAR_TEST, near, weight_sum)
    for k in range(64):
        dd[:, k * 128:(k + 1) * 128] = npole[k:k + 1, :] - dj

    def root_step(inverse, _, carry):
        t, lo, hi = carry
        tb = jnp.broadcast_to(t, (OWN, 128))
        zero = jnp.zeros((OWN, 128), F32)
        value, slope, dpsi = zero, zero, zero
        for k in range(64):
            q = inverse(dd[:, k * 128:(k + 1) * 128] - tb)
            w = nsq[k:k + 1, :] * q
            dw = w * q
            value = value + w
            slope = slope + dw
            dpsi = dpsi + jnp.where(w < 0.0, dw, 0.0)
        value = jnp.sum(value, axis=1, keepdims=True)
        slope = jnp.sum(slope, axis=1, keepdims=True)
        dpsi = jnp.sum(dpsi, axis=1, keepdims=True)
        dphi = jnp.maximum(slope - dpsi, 0.0)
        secular = 1.0 + rho * value
        is_below = secular < 0.0
        lo = jnp.where(is_below, t, lo)
        hi = jnp.where(is_below, hi, t)
        e = bracket - t
        lower = rho * t * t * dpsi
        upper = rho * e * e * dphi
        level = secular + rho * (t * dpsi - e * dphi)
        linear = level * bracket + lower + upper
        constant = lower * bracket
        side = level * bracket - lower + upper
        spread_root = jnp.sqrt(side * side + 4.0 * lower * upper)
        positive = linear > 0.0
        top = jnp.where(positive, 2.0 * constant, linear - spread_root)
        under = jnp.where(positive, linear + spread_root, 2.0 * level)
        fresh = top / jnp.where(under == 0.0, 1.0, under)
        usable = (fresh > 0.0) & (fresh < bracket)
        fresh = jnp.where(usable, jnp.minimum(jnp.maximum(fresh, lo), hi), 0.5 * (lo + hi))
        return fresh, lo, hi

    start = 0.5 * bracket
    nothing = jnp.zeros_like(start)
    rough = functools.partial(root_step, functools.partial(pl.reciprocal, approx=True))
    root, _, _ = lax.fori_loop(0, ROUGH_STEPS, rough, (start, nothing, bracket))
    for d in range(2):
        own_line(d, 1, 1 - d).wait_recv()
        own_line(d, 2, 1 - d).start()
    fine = functools.partial(root_step, reciprocal)
    root, _, _ = lax.fori_loop(0, FINE_STEPS, fine, (root, nothing, bracket))
    own_live = ljb[pl.ds(own_first, OWN), :] > 0.5
    buf3[r, :, :] = jnp.where(own_live, jnp.broadcast_to(root, (OWN, 128)), jnp.broadcast_to(start, (OWN, 128)))
    spread(buf3, NR, s3s, s3r, True)

    for d in range(2):
        own_line(d, 2, d).wait_recv()
        own_line(d, 3, d).start()
    for d in range(2):
        own_line(d, 2, 1 - d).wait_recv()
        over_x(1 + d, d).wait_recv()
        over_x(1 + d, 1 - d).wait_recv()
        x_line(d, 1, 1 - d).start()

    settle(buf3, NR, s3r)

    for i in range(4):
        poles = npole[pl.ds(4 * r + i, 1), :]
        total = jnp.ones((8, 128), F32)
        for g in range(OUT // 8):
            d_j = djb[g * 8:(g + 1) * 8, :]
            off = buf3[g // 2, (g % 2) * 8:(g % 2) * 8 + 8, :]
            gap = poles - d_j
            ratio = (gap - off) * reciprocal(jnp.where(gap == 0.0, 1.0, gap))
            total = total * jnp.where(ljb[g * 8:(g + 1) * 8, :] > 0.5, jnp.abs(ratio), 1.0)
        total = total[0:4] * total[4:8]
        total = total[0:2] * total[2:4]
        buf4[c, i:i + 1, :] = total[0:1] * total[1:2]
    for q in range(2):
        tile = jnp.concatenate([buf3[q * 8 + g, :, :] for g in range(8)], axis=0)
        buf4[c, 4 + q:5 + q, :] = jnp.transpose(tile)[0:1, :]
    buf4[c, 6:8, :] = jnp.ones((2, 128), F32)
    spread(buf4, NC, s4s, s4r, False)

    for d in range(2):
        over_x(3 + d, d).wait_recv()
        x_line(d, 2, d).start()
    for d in range(2):
        x_line(d, 1, 1 - d).wait_recv()
        x_line(d, 2, 1 - d).start()

    for b in range(16):
        line = lax.rem(x + 2 * (b // 8), NX)
        source = (b % 8) * NX + line
        row = h * NC + source
        alive_row = buf2[source, pl.ds(4 + h, 1), :] > 0.5
        kp[b:b + 1, :] = npole[pl.ds(row, 1), :]
        place = posn_ref[pl.ds(row, 1), :].astype(F32)
        kd[b:b + 1, :] = jnp.where(alive_row, -1.0, place)
    kp[16:128, :] = jnp.zeros((112, 128), F32)
    kd[16:128, :] = jnp.zeros((112, 128), F32)
    kpt = jnp.transpose(kp[...])
    kdt = jnp.transpose(kd[...])
    kp[...] = kpt
    kd[...] = kdt

    def inverse_gaps(group, block, offs):
        for q in range(2):
            d_j = pole_ref[pl.ds(2 * block + q, 1), :]
            alive_j = live_ref[pl.ds(2 * block + q, 1), :] > 0
            off = offs[q]
            index = (lax.broadcasted_iota(jnp.int32, (1, 128), 1) + (block * OUT + q * 128)).astype(F32)
            for b in range(16):
                col = kp[:, b:b + 1]
                gap = (col - d_j) - off
                inverse = jnp.where(col < FAR_TEST, reciprocal(gap), 0.0)
                same = jnp.where(kd[:, b:b + 1] == index, 1.0, 0.0)
                value = jnp.where(alive_j, inverse, same)
                hi = value.astype(BF16)
                lo = (value - hi.astype(F32)).astype(BF16)
                ch[b * 128:(b + 1) * 128, group * OUT + q * 128:group * OUT + (q + 1) * 128] = hi
                cl[b * 128:(b + 1) * 128, group * OUT + q * 128:group * OUT + (q + 1) * 128] = lo

    inverse_gaps(0, c, [buf4[c, 4:5, :], buf4[c, 5:6, :]])

    def square_group(g, _):
        first = pl.multiple_of(g * 8, 8)
        d_j = djb[pl.ds(first, 8), :]
        off = buf3[g // 2, pl.ds(pl.multiple_of(lax.rem(g, 2) * 8, 8), 8), :]
        for k in range(64):
            w = reciprocal((npole[k:k + 1, :] - d_j) - off)
            sq_ref[pl.ds(first, 8), k * 128:(k + 1) * 128] = w * w
        return 0

    lax.fori_loop(0, OUT // 8, square_group, 0)

    settle(buf4, NC, s4r)
    product = buf4[0, :, :]
    for k in range(1, NC):
        product = product * buf4[k, :, :]
    first_rows = lax.broadcasted_iota(jnp.int32, (8, 128), 0) < 4
    product = jnp.where(first_rows, product, 1.0)
    buf5[r, :, :] = jnp.sqrt(product / rho)
    spread(buf5, NR, s5s, s5r, True)

    for d in range(2):
        x_line(d, 2, d).wait_recv()
        x_line(d, 3, d).start()

    right = z * NX + lax.rem(x + 1, NX)
    left = z * NX + lax.rem(x + NX - 1, NX)
    for group, block in ((1, right), (2, left)):
        inverse_gaps(group, block, [buf4[block, 4:5, :], buf4[block, 5:6, :]])

    settle(buf5, NR, s5r)

    own_copy.wait()
    for k in range(2):
        own_line(k, 3, k).wait_recv()
        over_x(0, k).wait_recv()
        x_line(k, 2, 1 - k).wait_recv()
        x_line(k, 3, k).wait_recv()

    hats = []
    for b in range(16):
        line = lax.rem(x + 2 * (b // 8), NX)
        row = h * NC + (b % 8) * NX + line
        hat = buf5[h * 8 + b % 8, pl.ds(line, 1), :] * nsg[pl.ds(row, 1), :]
        hats.append(jnp.where(npole[pl.ds(row, 1), :] < FAR_TEST, hat, 1.0))

    def scaled(rows):
        for b in range(16):
            value = panel[b // 8, b % 8, rows, :] * hats[b]
            hi = value.astype(BF16)
            ah[rows, b * 128:(b + 1) * 128] = hi
            al[rows, b * 128:(b + 1) * 128] = (value - hi.astype(F32)).astype(BF16)

    def product_of(rows, group):
        cols = slice(group * OUT, (group + 1) * OUT)
        a_hi, a_lo = ah[rows, :], al[rows, :]
        c_hi, c_lo = ch[:, cols], cl[:, cols]
        return (
            jnp.dot(a_hi, c_lo, preferred_element_type=F32)
            + jnp.dot(a_lo, c_hi, preferred_element_type=F32)
        ) + jnp.dot(a_hi, c_hi, preferred_element_type=F32)

    def rows_of(side, piece):
        first = side * HALF_ROWS + piece * PIECE
        return slice(first, first + PIECE)

    def partial_copy(side, piece):
        rows = pl.ds(piece * PIECE, PIECE)
        return pltpu.make_async_remote_copy(
            src_ref=tx.at[side, rows], dst_ref=rx.at[side, rows], send_sem=rs.at[side, piece],
            recv_sem=rr.at[side, piece],
            device_id=col_dev(0, 1 if side == 0 else -1), device_id_type=MESH,
        )

    for piece in range(2):
        for side in range(2):
            rows = rows_of(side, piece)
            scaled(rows)
            tx[side, piece * PIECE:(piece + 1) * PIECE, :] = product_of(rows, 1 + side)
            partial_copy(side, piece).start()
    for piece in range(2):
        for side in range(2):
            rows = rows_of(side, piece)
            out_ref[rows, :] = product_of(rows, 0)

    hat_all = jnp.concatenate([buf5[k, 0:4, :] for k in range(16)], axis=0)
    nsg[...] = jnp.where(npole[...] < FAR_TEST, hat_all * hat_all, 0.0)

    def norm_group(g, _):
        first = pl.multiple_of(g * 8, 8)
        total = jnp.zeros((8, 128), F32)
        for k in range(64):
            total = total + nsg[k:k + 1, :] * sq_ref[pl.ds(first, 8), k * 128:(k + 1) * 128]
        norm_ref[pl.ds(first, 8), :] = total
        return 0

    lax.fori_loop(0, OUT // 8, norm_group, 0)
    scales = []
    for q in range(2):
        square = jnp.sum(jnp.transpose(norm_ref[q * 128:(q + 1) * 128, :]), axis=0, keepdims=True)
        alive_j = live_ref[pl.ds(2 * c + q, 1), :] > 0
        scales.append(jnp.where(alive_j, 1.0 / jnp.sqrt(jnp.where(alive_j, square, 1.0)), 1.0))
    scale = jnp.concatenate(scales, axis=1)

    for piece in range(2):
        for side in range(2):
            partial_copy(side, piece).wait_recv()
            rows = rows_of(side, piece)
            total = out_ref[rows, :] + rx[side, piece * PIECE:(piece + 1) * PIECE, :]
            out_ref[rows, :] = total * scale

    for q, owner in ((0, NR // 2 - 1), (1, NR // 2)):
        @pl.when(r == owner)
        def _():
            for k in range(1, NR):
                boundary_copy(q, k).wait_send()

    settle(buf2, NC, s2s)
    settle(buf3, NR, s3s)
    settle(buf4, NC, s4s)
    settle(buf5, NR, s5s)
    for k in range(2):
        for step in range(3):
            over_x(step, k).wait_send()
            for d in range(2):
                own_line(d, step, k).wait_send()
        own_line(k, 3, k).wait_send()
        over_x(3 + k, k).wait_send()
        x_line(k, 1, 1 - k).wait_send()
        x_line(k, 2, k).wait_send()
        x_line(k, 2, 1 - k).wait_send()
        x_line(k, 3, k).wait_send()
        for piece in range(2):
            partial_copy(k, piece).wait_send()


def shards(old_vectors, pole_values, live_mask, position, rank_weight):
    vmem = pl.BlockSpec(memory_space=pltpu.VMEM)
    v = pltpu.VMEM
    dma = pltpu.SemaphoreType.DMA
    one = dma(())
    return pl.pallas_call(
        kernel,
        out_shape=jax.ShapeDtypeStruct((ROWS, OUT), F32),
        in_specs=[vmem] * 4 + [pl.BlockSpec(memory_space=pltpu.SMEM)],
        out_specs=vmem,
        scratch_shapes=[
            v((2, NZ, ROWS, COLS), F32),
            v((2, 8, 128), F32), v((NC, 8, 128), F32), v((NR, OWN, 128), F32),
            v((NC, 8, 128), F32), v((NR, 8, 128), F32),
            v((OUT, 128), F32), v((OUT, 128), F32),
            v((128, 128), F32), v((128, 128), F32), v((8, 128), F32),
            v((64, 128), F32), v((64, 128), F32), v((64, 128), F32),
            v((OWN, 8192), F32), v((OWN, 128), F32),
            v((ROWS, 2048), BF16), v((ROWS, 2048), BF16),
            v((2048, 3 * OUT), BF16), v((2048, 3 * OUT), BF16),
            v((2, HALF_ROWS, OUT), F32), v((2, HALF_ROWS, OUT), F32), v((OUT, 128), F32),
            v((OUT, 8192), F32),
            dma((2,)), one, one, one, one, one, one, one, one,
            one, dma((2, 4, 2)), dma((2, 4, 2)), dma((5, 2)), dma((5, 2)),
            dma((2, 3, 2)), dma((2, 3, 2)), dma((2, 2)), dma((2, 2)), dma((NR - 1,)),
        ],
        compiler_params=pltpu.CompilerParams(
            collective_id=0, has_side_effects=True, vmem_limit_bytes=56 * 2**20
        ),
    )(
        old_vectors,
        pole_values.reshape(64, 128),
        live_mask.reshape(64, 128),
        position.reshape(64, 128),
        rank_weight,
    )


def solution(mesh):
    in_specs = (P("row", "col"), P(), P(), P(), P())
    return jax.shard_map(
        shards, mesh=mesh, in_specs=in_specs, out_specs=P("row", "col"), check_vma=False
    )
```
